256 devices in a mesh: node: 8 (over y, z_lo), gz: 32 (over z_hi, x, core).
Axes of the slice: x: 4, y: 4, z: 8 (z_hi: 4, z_lo: 2; z = z_hi * 2 + z_lo), core: 2. Of those that a mesh axis runs over, the one named last changes fastest.
Arguments:
- initial: float32 [2, 128, 128, 128], P(None, 'gz'), may hold values from -3 to 3
- feed_rate: float32 [128, 128, 128], P('gz'), may hold values from 2 to 4
Outputs:
- collocation: float32 [8, 2, 128, 128, 128], P('node', None, 'gz')
The draws below stay inside these ranges and needn't reach their ends.
All inputs are finite; a program needn't handle non-finite values.
Results may differ from the reference program's by a relative error of at most 0.0003.
Values sent between devices are 32-bit elements; how exact they have to be, the bound alone decides.
A program may use at most 64 MiB of HBM per device.

```python
import math
import jax
import jax.numpy as jnp
from jax import lax

M = 8
NX = 128
NY = 128
SWEEPS = 3
STEPS = 2
JACOBI = 4
NZ = 128


def steps_of(stream_key, shape, pieces, least, top_value):
    loudness, own = 1.0, jax.random.fold_in(stream_key, 6)
    for dim, blocks in pieces:
        steps = jnp.exp(jax.random.uniform(jax.random.fold_in(own, dim), (blocks,), jnp.float32, least / len(pieces), top_value / len(pieces)))
        loudness = loudness * jnp.repeat(steps, shape[dim] // blocks).reshape([-1 if axis == dim else 1 for axis in range(len(shape))])
    return loudness


def scatter_about(stream_key, extent, scale, limit, pieces=(), held_as=jnp.bfloat16):
    array = jax.random.normal(stream_key, extent, jnp.float32) * scale
    if len(pieces) > 0:
        array = steps_of(stream_key, extent, pieces, -0.22, 0.18) * array
    return jnp.clip(array, min=-limit, max=limit).astype(held_as)


def setup_inputs(seed: int = 0) -> dict:
    keys = jax.random.split(jax.random.key(seed), 3)
    initial = scatter_about(keys[0], (2, NZ, NX, NY), 0.5, 3.0, ((1, 32),), jnp.float32)
    feed_rate = jnp.clip(jnp.exp(math.log(4.0) - 0.6931472 * jax.random.uniform(keys[1], (NZ, NX, NY), jnp.float32) ** steps_of(keys[1], (NZ, NX, NY), ((0, 32),), -0.2, 0.2)), 2.0, 4.0)
    return dict(initial=initial, feed_rate=feed_rate)


time_step = 0.1
diffuse_u = 1.0
diffuse_v = 2.0


def legendre_pair(count, point):
    before = 1.0
    current = point
    for order in range(2, count + 1):
        after = ((2.0 * order - 1.0) * point * current - (order - 1.0) * before) / order
        before = current
        current = after
    return current, before


def radau_value(count, point):
    high, low = legendre_pair(count, point)
    return high - low


def radau_slope(count, point):
    high, low = legendre_pair(count, point)
    lower_high, lower_low = legendre_pair(count - 1, point)
    denom = point * point - 1.0
    slope_high = count * (point * high - low) / denom
    slope_low = (count - 1.0) * (point * lower_high - lower_low) / denom
    return slope_high - slope_low


def radau_tables(node_count):
    points = [1.0]
    for index in range(1, node_count):
        guess = math.cos(2.0 * math.pi * index / (2.0 * node_count - 1.0))
        for newton_index in range(100):
            guess = guess - radau_value(node_count, guess) / radau_slope(node_count, guess)
        points.append(guess)
    points = sorted(points)
    nodes = [(value + 1.0) / 2.0 for value in points]
    table = []
    for row in range(node_count):
        table.append([0.0] * node_count)
    for column in range(node_count):
        coeffs = [1.0]
        for other in range(node_count):
            if other != column:
                factor = 1.0 / (nodes[column] - nodes[other])
                shifted = [0.0] + coeffs
                scaled = [-nodes[other] * value for value in coeffs] + [0.0]
                coeffs = [(shifted[k] + scaled[k]) * factor for k in range(len(shifted))]
        for row in range(node_count):
            total = 0.0
            for power in range(len(coeffs)):
                total = total + coeffs[power] * nodes[row] ** (power + 1) / (power + 1.0)
            table[row][column] = total
    return nodes, table


def neighbour_sum(padded):
    center = padded[..., 1:-1, :, :]
    total = padded[..., 2:, :, :] + padded[..., :-2, :, :]
    flat = jnp.pad(center, [(0, 0)] * (center.ndim - 2) + [(1, 1), (1, 1)])
    total = total + flat[..., 2:, 1:-1] + flat[..., :-2, 1:-1]
    total = total + flat[..., 1:-1, 2:] + flat[..., 1:-1, :-2]
    return total


def pad_depth(field):
    return jnp.pad(field, [(0, 0)] * (field.ndim - 3) + [(1, 1), (0, 0), (0, 0)])


def reaction(iterate, feed_rate):
    upper = 1.0 + iterate[..., 0, :, :, :]
    lower = feed_rate + iterate[..., 1, :, :, :]
    cubic = upper * upper * lower
    first = 1.0 + cubic - (feed_rate + 1.0) * upper
    second = feed_rate * upper - cubic
    return jnp.stack((first, second), axis=-4)


def reference(initial, feed_rate):
    nodes, weights = radau_tables(M)
    weights = jnp.asarray(weights, jnp.float32)
    nodes = jnp.asarray(nodes, jnp.float32)
    diffusion = jnp.asarray([diffuse_u, diffuse_v], jnp.float32)[:, None, None, None]
    anchor = initial
    iterate = jnp.broadcast_to(anchor, (M,) + anchor.shape)
    for step_index in range(STEPS):
        iterate = jnp.broadcast_to(anchor, (M,) + anchor.shape)
        for sweep_index in range(SWEEPS):
            stiffness = (nodes / (sweep_index + 1.0))[:, None, None, None, None] * diffusion
            laplace = neighbour_sum(pad_depth(iterate)) - 6.0 * iterate
            slopes = diffusion * laplace + time_step * reaction(iterate, feed_rate)
            integral = jnp.einsum('mj,jsabc->msabc', weights, slopes, precision=lax.Precision.HIGHEST)
            right_side = anchor + integral - stiffness * laplace
            current = iterate
            for jacobi_index in range(JACOBI):
                current = (right_side + stiffness * neighbour_sum(pad_depth(current))) / (1.0 + 6.0 * stiffness)
            iterate = current
        anchor = iterate[M - 1]
    return iterate
```

```python
import math

import jax
import jax.numpy as jnp
import ml_dtypes
import numpy as np
from jax import lax
from jax.experimental import pallas as pl
from jax.experimental.pallas import tpu as pltpu
from jax.sharding import PartitionSpec as P

MESH = pl.DeviceIdType.MESH
M = 8
SLABS, STRIPS = 32, 8
OWN_Z, OWN_X = 4, 16
Z_AT, X_AT = 12, 16
WIDE = 128


def legendre_pair(count, point):
    before = 1.0
    current = point
    for order in range(2, count + 1):
        after = ((2.0 * order - 1.0) * point * current - (order - 1.0) * before) / order
        before = current
        current = after
    return (current, before)


def radau_value(count, point):
    high, low = legendre_pair(count, point)
    return high - low


def radau_slope(count, point):
    high, low = legendre_pair(count, point)
    lower_high, lower_low = legendre_pair(count - 1, point)
    denom = point * point - 1.0
    slope_high = count * (point * high - low) / denom
    slope_low = (count - 1.0) * (point * lower_high - lower_low) / denom
    return slope_high - slope_low


def radau_tables(node_count):
    points = [1.0]
    for index in range(1, node_count):
        guess = math.cos(2.0 * math.pi * index / (2.0 * node_count - 1.0))
        for newton_index in range(100):
            guess = guess - radau_value(node_count, guess) / radau_slope(node_count, guess)
        points.append(guess)
    points = sorted(points)
    nodes = [(value + 1.0) / 2.0 for value in points]
    table = []
    for row in range(node_count):
        table.append([0.0] * node_count)
    for column in range(node_count):
        coeffs = [1.0]
        for other in range(node_count):
            if other != column:
                factor = 1.0 / (nodes[column] - nodes[other])
                shifted = [0.0] + coeffs
                scaled = [-nodes[other] * value for value in coeffs] + [0.0]
                coeffs = [(shifted[k] + scaled[k]) * factor for k in range(len(shifted))]
        for row in range(node_count):
            total = 0.0
            for power in range(len(coeffs)):
                total = total + coeffs[power] * nodes[row] ** (power + 1) / (power + 1.0)
            table[row][column] = total
    return (nodes, table)


def tables():
    nodes, weights = radau_tables(M)
    t, q = np.asarray(nodes), np.asarray(weights)
    k = np.arange(1, WIDE + 1)
    sine = np.sqrt(2.0 / (WIDE + 1)) * np.sin(np.pi * np.outer(k, k) / (WIDE + 1))
    index, rows = {}, []

    def add(name, column):
        index[name] = len(rows)
        rows.append(np.broadcast_to(column[:, None], (8, WIDE)))

    index["lam"] = 0
    rows.append(np.broadcast_to(2.0 * np.cos(np.pi * k / (WIDE + 1))[None, :], (8, WIDE)))
    for s, nu in ((0, 1.0), (1, 2.0)):
        c = t * nu
        i = 1.0 / (1.0 + 6.0 * c)
        a = c * i
        for p in range(4):
            add(("A", s, p), a**p * i * ((1.0 - 0.1 * t) if s == 0 else 1.0))
            add(("N", s, p), a**p * i * t * (1.0 if s == 0 else -1.0))
        add(("A", s, 4), a**4)
        for sweep in (2, 3):
            c = t * nu / sweep
            i = 1.0 / (1.0 + 6.0 * c)
            add(("c", s, sweep), c)
            add(("i", s, sweep), i)
            add(("a", s, sweep), c * i)
    for j in range(M):
        add(("q", j), q[:, j])
    return np.concatenate(rows, 0).astype(np.float32), index, sine


COEF, INDEX, SINE = tables()


def wide(matrix):
    high = matrix.astype(ml_dtypes.bfloat16)
    low = (matrix - high.astype(np.float64)).astype(ml_dtypes.bfloat16)
    return np.block([[high, low], [high, np.zeros_like(low)]]).astype(ml_dtypes.bfloat16)


def transform(v, matrix):
    high = v.astype(jnp.bfloat16)
    low = (v - high.astype(jnp.float32)).astype(jnp.bfloat16)
    both = jnp.dot(jnp.concatenate([high, low], 1), matrix[...], preferred_element_type=jnp.float32)
    return both[:, :WIDE] + both[:, WIDE:]


def total(terms):
    while len(terms) > 1:
        odd = [terms[-1]] if len(terms) % 2 else []
        terms = [terms[i] + terms[i + 1] for i in range(0, len(terms) - 1, 2)] + odd
    return terms[0]


class Stack:
    def __init__(self, ref, z0, nz, x0, nx):
        self.ref, self.z0, self.nz, self.x0, self.nx = ref, z0, nz, x0, nx

    def at(self, s, z, x):
        return pl.multiple_of(((s * self.nz + (z - self.z0)) * self.nx + (x - self.x0)) * 8, 8)

    def get(self, s, z, x):
        return self.ref[pl.ds(self.at(s, z, x), 8), :]

    def put(self, s, z, x, v):
        self.ref[pl.ds(self.at(s, z, x), 8), :] = v

    def row(self, s, z, x, f):
        return jnp.broadcast_to(self.ref[pl.ds(self.at(s, z, x) + f, 1), :], (8, WIDE))

    def line(self, s, z, x, n):
        return self.ref[pl.ds(self.at(s, z, x), n * 8), :]


def span(depth):
    return (Z_AT - depth, OWN_Z + 2 * depth, X_AT - depth, OWN_X + 2 * depth)


def volume(depth):
    return 2 * (OWN_Z + 2 * depth) * (OWN_X + 2 * depth) * 8


class Device:
    def __init__(self, refs, g, k):
        self.__dict__.update(refs)
        self.g, self.k = g, k

    def co(self, name):
        i = INDEX[name]
        return self.coef[i * 8 : (i + 1) * 8, :]

    def zero_edges(self, stack, parts):
        for edge, x in ((0, X_AT - 1), (STRIPS - 1, X_AT + OWN_X)):

            @pl.when(self.k == edge)
            def _():
                def body(z, _):
                    for s in range(parts):
                        stack.put(s, z, x, jnp.zeros((8, WIDE), jnp.float32))
                    return 0

                lax.fori_loop(stack.z0, stack.z0 + stack.nz, body, 0)

        for i in range(3):
            for edge, z in ((i, Z_AT - 4 * i - 1), (SLABS - 1 - i, Z_AT + OWN_Z + 4 * i)):
                if stack.z0 <= z < stack.z0 + stack.nz:

                    @pl.when(self.g == edge)
                    def _():
                        for s in range(parts):
                            stack.ref[pl.ds(stack.at(s, z, stack.x0), stack.nx * 8), :] = jnp.zeros(
                                (stack.nx * 8, WIDE), jnp.float32
                            )

    def load(self, blocks, first, stack):
        def body(slot, _):
            b = slot * 3
            x = jnp.concatenate([blocks[b + i, 0:2].reshape(128, WIDE) for i in range(3)], 0)
            y = transform(x, self.sine)
            real, spec = (x, y) if first else (y, x)
            n = []
            for i in range(3):
                p, q = real[i * 128 : i * 128 + 64], real[i * 128 + 64 : i * 128 + 128]
                feed = self.held[b + i, 2].reshape(64, WIDE)
                n.append((1.0 + p) * (q + p * (feed + q)))
            n = transform(jnp.concatenate(n, 0), self.sine_tenth)
            for i in range(3):
                for layer in range(4):
                    for t in range(2):
                        at = stack.at(0, slot * 4 + layer, i * 16 + t * 8)
                        r = layer * 16 + t * 8
                        for f, v in (
                            (0, spec[i * 128 + r : i * 128 + r + 8]),
                            (1, spec[i * 128 + 64 + r : i * 128 + 64 + r + 8]),
                            (2, n[i * 64 + r : i * 64 + r + 8]),
                        ):
                            stack.ref[pl.ds(at + f, 8, stride=8), :] = v
            return 0

        lax.fori_loop(0, 7, body, 0)

    def apply_s(self, src, dst):
        lam = self.co("lam")

        def body(z, _):
            for x0 in range(dst.x0, dst.x0 + dst.nx, 8):
                xs = range(x0, min(x0 + 8, dst.x0 + dst.nx))
                row = {x: src.get(0, z, x) for x in range(xs[0] - 1, xs[-1] + 2)}
                for x in xs:
                    zx = (row[x - 1] + row[x + 1]) + (src.get(0, z - 1, x) + src.get(0, z + 1, x))
                    dst.put(0, z, x, zx + lam * row[x])
            return 0

        lax.fori_loop(dst.z0, dst.z0 + dst.nz, body, 0)

    def combine(self, powers, out):
        ca = [[self.co(("A", s, p)) for p in range(5)] for s in range(2)]
        cn = [[self.co(("N", s, p)) for p in range(4)] for s in range(2)]

        def body(z, _):
            for x in range(out.x0, out.x0 + out.nx):
                n = [powers[p].row(0, z, x, 2) for p in range(4)]
                for s in range(2):
                    terms = [ca[s][p] * powers[p].row(0, z, x, s) for p in range(5)]
                    out.put(s, z, x, total(terms + [cn[s][p] * n[p] for p in range(4)]))
            return 0

        lax.fori_loop(out.z0, out.z0 + out.nz, body, 0)

    def rates(self, u, anchor, right, out, sweep):
        lam = self.co("lam")
        a, c, inv = [[self.co((name, s, sweep)) for s in range(2)] for name in "aci"]
        weights = [self.co(("q", j)) for j in range(M)]
        nx, x0 = right.nx, right.x0
        lam6, lam61 = lam - 6.0, lam - 6.1
        rate = Stack(self.rate, 0, 2, x0, nx)

        def body(i, _):
            z0 = right.z0 + 2 * i
            real = transform(
                jnp.concatenate([u.line(s, z0 + w, x0, nx) for s in range(2) for w in range(2)], 0), self.sine
            )
            feed = []
            for w in range(2):
                z = z0 + w
                for x in range(x0, x0 + nx):
                    line = self.held[(z // 4) * 3 + x // 16, 2, z % 4, pl.ds(x % 16, 1), :]
                    feed.append(jnp.broadcast_to(line, (8, WIDE)))
            feed = jnp.concatenate(feed, 0)
            p, q = real[: 2 * nx * 8], real[2 * nx * 8 :]
            self.modes[0 : 2 * nx * 8, :] = transform((1.0 + p) * (q + p * (feed + q)), self.sine_tenth)
            for w in range(2):
                z = z0 + w
                for x in range(x0, x0 + nx):
                    shifted, laplace = [], []
                    for s in range(2):
                        own = u.get(s, z, x)
                        zx = (u.get(s, z, x - 1) + u.get(s, z, x + 1)) + (u.get(s, z - 1, x) + u.get(s, z + 1, x))
                        shifted.append(zx + lam * own)
                        laplace.append(zx + lam6 * own)
                        if s == 0:
                            drift = zx + lam61 * own
                    at = (w * nx + x - x0) * 8
                    n = self.modes[at : at + 8, :]
                    rate.put(0, w, x, drift + n)
                    rate.put(1, w, x, 2.0 * laplace[1] - n)
                    for s in range(2):
                        integral = total([weights[j] * rate.row(s, w, x, j) for j in range(M)])
                        r = inv[s] * ((anchor.row(0, z, x, s) - c[s] * laplace[s]) + integral)
                        right.put(s, z, x, r)
                        out.put(s, z, x, r + a[s] * shifted[s])
            return 0

        lax.fori_loop(0, right.nz // 2, body, 0)

    def jacobi(self, src, right, dst, sweep):
        lam = self.co("lam")
        a = [self.co(("a", s, sweep)) for s in range(2)]

        def body(z, _):
            for x0 in range(dst.x0, dst.x0 + dst.nx, 7):
                xs = range(x0, min(x0 + 7, dst.x0 + dst.nx))
                for s in range(2):
                    row = {x: src.get(s, z, x) for x in range(xs[0] - 1, xs[-1] + 2)}
                    for x in xs:
                        zx = (row[x - 1] + row[x + 1]) + (src.get(s, z - 1, x) + src.get(s, z + 1, x))
                        dst.put(s, z, x, right.get(s, z, x) + a[s] * (zx + lam * row[x]))
            return 0

        lax.fori_loop(dst.z0, dst.z0 + dst.nz, body, 0)

    def step(self, blocks, first):
        powers = [Stack(self.power[0], 0, 28, 0, 48)]
        powers += [Stack(self.power[i], i, 28 - 2 * i, 4 + i, 40 - 2 * i) for i in range(1, 5)]
        self.load(blocks, first, powers[0])
        for i in range(4):
            self.zero_edges(powers[i], 1)
            self.apply_s(powers[i], powers[i + 1])
        u = Stack(self.state[0], *span(8))
        self.combine(powers, u)
        for sweep, depth in ((2, 8), (3, 4)):
            right, out = Stack(self.state[1], *span(depth - 1)), Stack(self.state[2], *span(depth - 1))
            self.zero_edges(u, 2)
            self.rates(u, powers[0], right, out, sweep)
            for d, place in ((depth - 2, 3), (depth - 3, 2), (depth - 4, 3)):
                u = Stack(self.state[place], *span(d))
                self.zero_edges(out, 2)
                self.jacobi(out, right, u, sweep)
                out = u
        return u


def strip_of(node):
    y = node // 2
    return 2 * y + (node + y) % 2


class Links:
    def __init__(self):
        self.sent = []

    def send(self, when, copy):
        @pl.when(when)
        def _():
            copy.start()

        self.sent.append((when, copy))

    def finish(self):
        for when, copy in self.sent:

            @pl.when(when)
            def _():
                copy.wait_send()


def remote(src, dst, sent, got, node, g):
    return pltpu.make_async_remote_copy(
        src_ref=src, dst_ref=dst, send_sem=sent, recv_sem=got, device_id=(node, g), device_id_type=MESH
    )


def arrive(when, copy):
    @pl.when(when)
    def _():
        copy.wait_recv()


def exchange(held, sems, n, g, k, own_parts, strips_too):
    zs, zr, xs, xr, ss, sr = sems
    links = Links()
    tau = 2 * (g % 2) - 1
    partner = g - tau
    low, high = k > 0, k < STRIPS - 1

    def inside(i):
        return jnp.logical_and(i >= 0, i < SLABS)

    def block(slot, strip):
        return held.at[slot * 3 + strip]

    for d, away in ((1, tau), (2, -2 * tau), (3, 3 * tau)):
        for i, (src, part) in enumerate(own_parts):
            dst = held.at[(3 - away) * 3 + 1, part]
            copy = remote(src, dst, zs.at[d - 1, i], zr.at[d - 1, i], n, g + away)
            links.send(inside(g + away), copy)

    def along_x(j, there):
        slot = 3 + tau * j
        for way, (ok, to, strip) in enumerate(((high, k + 1, 0), (low, k - 1, 2))):
            copy = remote(block(slot, 1), block(slot, strip), xs.at[j, way], xr.at[j, way], strip_of(to), g)
            links.send(jnp.logical_and(ok, there), copy)

    def swap(j, strip, there):
        copy = remote(
            block(3 + tau * j, strip), block(3 + tau * (j + 1), strip), ss.at[j, strip], sr.at[j, strip], n, partner
        )
        links.send(there, copy)

    always = g >= 0
    swap(0, 1, always)
    if strips_too:
        along_x(0, always)
    else:
        swap(0, 0, low)
        swap(0, 2, high)
    for j in (1, 2, 3):
        there = inside(g + tau * j)
        slot = 3 + tau * j
        for i, (src, part) in enumerate(own_parts):
            arrive(there, remote(src, held.at[slot * 3 + 1, part], zs.at[j - 1, i], zr.at[j - 1, i], n, partner))
        along_x(j, there)
        if j < 3:
            swap(j, 1, there)
    for j in (0, 1, 2, 3):
        there = inside(g + tau * j)
        slot = 3 + tau * j
        for way, (ok, strip) in enumerate(((low, 0), (high, 2))):
            when = jnp.logical_and(ok, there)
            if j > 0 or strips_too:
                arrive(when, remote(block(slot, strip), block(slot, strip), xs.at[j, way], xr.at[j, way], n, partner))
                if j < 3:
                    swap(j, strip, when)
    for j in (0, 1, 2):
        there = inside(g - tau * (j + 1))
        for strip, ok in ((0, low), (1, always), (2, high)):
            slot = 3 - tau * (j + 1)
            got = remote(block(slot, strip), block(slot, strip), ss.at[j, strip], sr.at[j, strip], n, partner)
            arrive(jnp.logical_and(ok, there), got)
    links.finish()


def kernel(initial, feed, sine, sine_tenth, coef, out, held, later, rows, sending, *scratch):
    power, state, (rate, modes), sems = scratch[0:5], scratch[5:9], scratch[9:11], scratch[11:]
    own_sem, first_sems, second_sems, (send_sem, recv_sem) = sems[0], sems[1:7], sems[7:13], sems[13:15]
    n, g = lax.axis_index("node"), lax.axis_index("gz")
    k = strip_of(n)
    tau = 2 * (g % 2) - 1

    barrier = pltpu.get_barrier_semaphore()
    count = M - 1
    for j in range(1, M):
        pl.semaphore_signal(barrier, inc=1, device_id=((n + j) % M, g), device_id_type=MESH)
    for away in (-2 * tau, -tau, tau, 2 * tau, 3 * tau):
        there = jnp.logical_and(g + away >= 0, g + away < SLABS)
        count = count + jnp.where(there, 1, 0)

        @pl.when(there)
        def _():
            pl.semaphore_signal(barrier, inc=1, device_id=(n, g + away), device_id_type=MESH)

    own = []
    for strip, ok in ((0, k > 0), (1, k >= 0), (2, k < STRIPS - 1)):
        rows_of = pl.ds(pl.multiple_of(OWN_X * (k + strip - 1), 16), OWN_X)
        for i, (src, part) in enumerate(((initial.at[:, :, rows_of, :], pl.ds(0, 2)), (feed.at[:, rows_of, :], 2))):
            own.append((ok, pltpu.make_async_copy(src, held.at[9 + strip, part], own_sem.at[strip, i])))
    for ok, copy in own:

        @pl.when(ok)
        def _():
            copy.start()

    pl.semaphore_wait(barrier, count)
    for ok, copy in own:

        @pl.when(ok)
        def _():
            copy.wait()

    exchange(held, first_sems, n, g, k, ((held.at[10, pl.ds(0, 3)], pl.ds(0, 3)),), False)

    refs = dict(held=held, sine=sine, sine_tenth=sine_tenth, coef=coef, power=power, state=state, rate=rate, modes=modes)
    device = Device(refs, g, k)
    u = device.step(held, True)
    for s in range(2):
        for z in range(OWN_Z):
            for t in range(2):
                at = u.at(s, Z_AT + z, X_AT + 8 * t)
                later[10, s, z, 8 * t : 8 * t + 8, :] = u.ref[pl.ds(at + M - 1, 8, stride=8), :]
    exchange(later, second_sems, n, g, k, ((later.at[10, pl.ds(0, 2)], pl.ds(0, 2)),), True)

    u = device.step(later, False)
    rows[...] = transform(u.ref[0 : volume(0), :], sine)

    def spread(m, _):
        for s in range(2):
            for z in range(OWN_Z):
                for t in range(2):
                    at = ((s * OWN_Z + z) * OWN_X + 8 * t) * 8
                    sending[m, s, z, 8 * t : 8 * t + 8, :] = rows[pl.ds(at + m, 8, stride=8), :]
        return 0

    lax.fori_loop(0, M, spread, 0)
    here = out.at[0, :, :, pl.ds(pl.multiple_of(OWN_X * k, 16), OWN_X), :]
    copies = []
    for j in range(1, M):
        to = (n + j) % M
        copy = remote(sending.at[to], here, send_sem.at[j], recv_sem.at[j], to, g)
        copy.start()
        copies.append(copy)
    local = pltpu.make_async_copy(sending.at[n], here, send_sem.at[0])
    local.start()
    local.wait()
    for copy in copies:
        copy.wait()


def on_device(initial, feed):
    sem = pltpu.SemaphoreType.DMA
    f32 = jnp.float32
    exchanges = [sem((3, 1)), sem((3, 1)), sem((4, 2)), sem((4, 2)), sem((3, 3)), sem((3, 3))]
    scratch = [
        pltpu.VMEM((21, 3, OWN_Z, OWN_X, WIDE), f32),
        pltpu.VMEM((21, 2, OWN_Z, OWN_X, WIDE), f32),
        pltpu.VMEM((volume(0), WIDE), f32),
        pltpu.VMEM((M, 2, OWN_Z, OWN_X, WIDE), f32),
        pltpu.VMEM((28 * 48 * 8, WIDE), f32),
    ]
    scratch += [pltpu.VMEM(((28 - 2 * i) * (40 - 2 * i) * 8, WIDE), f32) for i in range(1, 5)]
    scratch += [pltpu.VMEM((volume(d), WIDE), f32) for d in (8, 7, 7, 6)]
    scratch += [pltpu.VMEM((2 * 2 * 30 * 8, WIDE), f32), pltpu.VMEM((2 * 30 * 8, WIDE), f32)]
    scratch += [sem((3, 2))] + exchanges + exchanges + [sem((M,)), sem((M,))]
    vmem, anywhere = pl.BlockSpec(memory_space=pltpu.VMEM), pl.BlockSpec(memory_space=pl.ANY)
    return pl.pallas_call(
        kernel,
        out_shape=jax.ShapeDtypeStruct((1, 2, OWN_Z, WIDE, WIDE), f32),
        in_specs=[anywhere, anywhere, vmem, vmem, vmem],
        out_specs=anywhere,
        scratch_shapes=scratch,
        compiler_params=pltpu.CompilerParams(
            collective_id=0, has_side_effects=True, vmem_limit_bytes=60 * 1024 * 1024
        ),
    )(initial, feed, jnp.asarray(wide(SINE)), jnp.asarray(wide(0.1 * SINE)), jnp.asarray(COEF))


def solution(mesh):
    in_specs = (P(None, "gz", None, None), P("gz", None, None))
    out_specs = P("node", None, "gz", None, None)
    return jax.shard_map(on_device, mesh=mesh, in_specs=in_specs, out_specs=out_specs, check_vma=False)
```

```python
import math

import jax
import jax.numpy as jnp
import ml_dtypes
import numpy as np
from jax import lax
from jax.experimental import pallas as pl
from jax.experimental.pallas import tpu as pltpu
from jax.sharding import PartitionSpec as P

MESH = pl.DeviceIdType.MESH
M = 8
SLABS, STRIPS = 32, 8
OWN_Z, OWN_X = 4, 16
Z_AT, X_AT = 12, 16
SLOTS = 6
WIDE = 128


def legendre_pair(count, point):
    before = 1.0
    current = point
    for order in range(2, count + 1):
        after = ((2.0 * order - 1.0) * point * current - (order - 1.0) * before) / order
        before = current
        current = after
    return (current, before)


def radau_value(count, point):
    high, low = legendre_pair(count, point)
    return high - low


def radau_slope(count, point):
    high, low = legendre_pair(count, point)
    lower_high, lower_low = legendre_pair(count - 1, point)
    denom = point * point - 1.0
    slope_high = count * (point * high - low) / denom
    slope_low = (count - 1.0) * (point * lower_high - lower_low) / denom
    return slope_high - slope_low


def radau_tables(node_count):
    points = [1.0]
    for index in range(1, node_count):
        guess = math.cos(2.0 * math.pi * index / (2.0 * node_count - 1.0))
        for newton_index in range(100):
            guess = guess - radau_value(node_count, guess) / radau_slope(node_count, guess)
        points.append(guess)
    points = sorted(points)
    nodes = [(value + 1.0) / 2.0 for value in points]
    table = []
    for row in range(node_count):
        table.append([0.0] * node_count)
    for column in range(node_count):
        coeffs = [1.0]
        for other in range(node_count):
            if other != column:
                factor = 1.0 / (nodes[column] - nodes[other])
                shifted = [0.0] + coeffs
                scaled = [-nodes[other] * value for value in coeffs] + [0.0]
                coeffs = [(shifted[k] + scaled[k]) * factor for k in range(len(shifted))]
        for row in range(node_count):
            total = 0.0
            for power in range(len(coeffs)):
                total = total + coeffs[power] * nodes[row] ** (power + 1) / (power + 1.0)
            table[row][column] = total
    return (nodes, table)


def tables():
    nodes, weights = radau_tables(M)
    t, q = np.asarray(nodes), np.asarray(weights)
    k = np.arange(1, WIDE + 1)
    sine = np.sqrt(2.0 / (WIDE + 1)) * np.sin(np.pi * np.outer(k, k) / (WIDE + 1))
    index, rows = {}, []

    def add(name, column):
        index[name] = len(rows)
        rows.append(np.broadcast_to(column[:, None], (8, WIDE)))

    index["lam"] = 0
    rows.append(np.broadcast_to(2.0 * np.cos(np.pi * k / (WIDE + 1))[None, :], (8, WIDE)))
    for s, nu in ((0, 1.0), (1, 2.0)):
        c = t * nu
        i = 1.0 / (1.0 + 6.0 * c)
        a = c * i
        for p in range(4):
            add(("A", s, p), a**p * i * ((1.0 - 0.1 * t) if s == 0 else 1.0))
            add(("N", s, p), a**p * i * t * (1.0 if s == 0 else -1.0))
        add(("A", s, 4), a**4)
        for sweep in (2, 3):
            c = t * nu / sweep
            i = 1.0 / (1.0 + 6.0 * c)
            add(("i", s, sweep), i)
            add(("a", s, sweep), c * i)
            for j in range(M):
                add(("q", s, sweep, j), i * q[:, j])
    return np.concatenate(rows, 0).astype(np.float32), index, sine


COEF, INDEX, SINE = tables()


def wide(matrix):
    high = matrix.astype(ml_dtypes.bfloat16)
    low = (matrix - high.astype(np.float64)).astype(ml_dtypes.bfloat16)
    return np.block([[high, low], [high, np.zeros_like(low)]]).astype(ml_dtypes.bfloat16)


def transform(v, matrix):
    high = v.astype(jnp.bfloat16)
    low = (v - high.astype(jnp.float32)).astype(jnp.bfloat16)
    both = jnp.dot(jnp.concatenate([high, low], 1), matrix[...], preferred_element_type=jnp.float32)
    return both[:, :WIDE] + both[:, WIDE:]


def total(terms):
    while len(terms) > 1:
        odd = [terms[-1]] if len(terms) % 2 else []
        terms = [terms[i] + terms[i + 1] for i in range(0, len(terms) - 1, 2)] + odd
    return terms[0]


class Stack:
    def __init__(self, ref, z0, nz, x0, nx):
        self.ref, self.z0, self.nz, self.x0, self.nx = ref, z0, nz, x0, nx
        self.lines = {}

    def start(self, s, z):
        if isinstance(z, int):
            return (s * self.nz + z - self.z0) * self.nx * 8
        if (s, id(z)) not in self.lines:
            self.lines[s, id(z)] = z, (z + (s * self.nz - self.z0)) * (self.nx * 8)
        return self.lines[s, id(z)][1]

    def at(self, s, z, x, dz=0):
        return pl.multiple_of(self.start(s, z) + (dz * self.nx + x - self.x0) * 8, 8)

    def get(self, s, z, x, dz=0):
        return self.ref[pl.ds(self.at(s, z, x, dz), 8), :]

    def put(self, s, z, x, v):
        self.ref[pl.ds(self.at(s, z, x), 8), :] = v

    def row(self, s, z, x, f):
        return jnp.broadcast_to(self.ref[pl.ds(self.at(s, z, x) + f, 1), :], (8, WIDE))

    def line(self, s, z, x, n):
        return self.ref[pl.ds(self.at(s, z, x), n * 8), :]


def span(depth):
    layers = OWN_Z + (2 * depth if depth < 4 else depth + (depth - 4))
    return (Z_AT - depth, layers, X_AT - depth, OWN_X + 2 * depth)


def volume(depth):
    _, layers, _, columns = span(depth)
    return 2 * layers * columns * 8


class Device:
    def __init__(self, refs, g, k):
        self.__dict__.update(refs)
        self.k, self.core = k, g % 2
        self.far = g // 2 + self.core * (SLABS // 2 - 1 - 2 * (g // 2))

    def zero_packed(self, stack):
        for edge, x in ((0, X_AT - 1), (STRIPS - 1, X_AT + OWN_X)):

            @pl.when(self.k == edge)
            def _():
                def body(z, _):
                    stack.put(0, z, x, jnp.zeros((8, WIDE), jnp.float32))
                    return 0

                lax.fori_loop(stack.z0, stack.z0 + stack.nz, body, 0)

        for edge, z in ((0, Z_AT - 1), (1, Z_AT - 9), (SLABS // 2 - 1, Z_AT + 8)):

            @pl.when(self.far == edge)
            def _():
                for half in range(2):
                    line = z - 8 * half
                    if stack.z0 <= line < stack.z0 + stack.nz:

                        def body(x, _):
                            stack.ref[pl.ds(stack.at(0, line, x) + 4 * half, 4), :] = jnp.zeros((4, WIDE), jnp.float32)
                            return 0

                        lax.fori_loop(stack.x0, stack.x0 + stack.nx, body, 0)

    def natural(self, layer):
        return layer + self.core * (OWN_Z - 1 - 2 * layer)

    def co(self, name):
        i = INDEX[name]
        return self.coef[i * 8 : (i + 1) * 8, :]

    def zero_edges(self, stack, species=(0, 1), lines=None):
        first, last = lines or (stack.z0, stack.z0 + stack.nz)
        for edge, x in ((0, X_AT - 1), (STRIPS - 1, X_AT + OWN_X)):

            @pl.when(self.k == edge)
            def _():
                def body(z, _):
                    for s in species:
                        stack.put(s, z, x, jnp.zeros((8, WIDE), jnp.float32))
                    return 0

                lax.fori_loop(first, last, body, 0)

        for edge, z in ((0, Z_AT - 1), (1, Z_AT - 9), (SLABS // 2 - 1, Z_AT + 8)):
            if first <= z < last:

                @pl.when(self.far == edge)
                def _():
                    for s in species:
                        stack.ref[pl.ds(stack.at(s, z, stack.x0), stack.nx * 8), :] = jnp.zeros(
                            (stack.nx * 8, WIDE), jnp.float32
                        )

    def load(self, blocks, first, stack, slot):
        b = slot * 3
        x = jnp.concatenate([blocks[b + i, 0:2].reshape(128, WIDE) for i in range(3)], 0)
        y = transform(x, self.sine)
        real, spec = (x, y) if first else (y, x)
        n = []
        for i in range(3):
            p, q = real[i * 128 : i * 128 + 64], real[i * 128 + 64 : i * 128 + 128]
            feed = self.held[b + i, 2].reshape(64, WIDE)
            n.append((1.0 + p) * (q + p * (feed + q)))
        n = transform(jnp.concatenate(n, 0), self.sine_tenth)
        for half in range(2):
            if not 0 <= slot - 2 * half < 4:
                continue
            for i in range(3):
                for layer in range(4):
                    for t in range(2):
                        z = (slot - 2 * half) * 4 + self.natural(layer)
                        at = stack.at(0, z, i * 16 + t * 8) + 4 * half
                        r = layer * 16 + t * 8
                        for f, v in (
                            (0, spec[i * 128 + r : i * 128 + r + 8]),
                            (1, spec[i * 128 + 64 + r : i * 128 + 64 + r + 8]),
                            (2, n[i * 64 + r : i * 64 + r + 8]),
                        ):
                            stack.ref[pl.ds(at + f, 8, stride=8), :] = v

    def apply_s(self, src, dst):
        lam = self.co("lam")

        def body(z, _):
            for x0 in range(dst.x0, dst.x0 + dst.nx, 8):
                xs = range(x0, min(x0 + 8, dst.x0 + dst.nx))
                row = {x: src.get(0, z, x) for x in range(xs[0] - 1, xs[-1] + 2)}
                for x in xs:
                    zx = (row[x - 1] + row[x + 1]) + (src.get(0, z, x, -1) + src.get(0, z, x, 1))
                    dst.put(0, z, x, zx + lam * row[x])
            return 0

        lax.fori_loop(dst.z0, dst.z0 + dst.nz, body, 0)

    def combine(self, powers, out):
        ca = [[self.co(("A", s, p)) for p in range(5)] for s in range(2)]
        cn = [[self.co(("N", s, p)) for p in range(4)] for s in range(2)]
        def body(z, _):
            half = lax.div(z - 4, 8)
            line, row = z - 8 * half, 4 * half
            for x in range(out.x0, out.x0 + out.nx):
                n = [powers[p].row(0, line, x, row + 2) for p in range(4)]
                for s in range(2):
                    terms = [ca[s][p] * powers[p].row(0, line, x, row + s) for p in range(5)]
                    out.put(s, z, x, total(terms + [cn[s][p] * n[p] for p in range(4)]))
            return 0

        lax.fori_loop(out.z0, out.z0 + out.nz, body, 0)

    def rates(self, u, anchor, right, out, sweep, pause=None):
        lam = self.co("lam")
        a, inv = [[self.co((name, s, sweep)) for s in range(2)] for name in "ai"]
        a6 = [6.0 * a[s] for s in range(2)]
        weights = [[self.co(("q", s, sweep, j)) for j in range(M)] for s in range(2)]
        nx, x0, lines = right.nx, right.x0, right.nz
        lam6, lam61 = lam - 6.0, lam - 6.1
        rate = Stack(self.rate, 0, 1, x0, nx)

        def nonlinear(i, place):
            z = right.z0 + lax.rem(i, lines)
            real = transform(jnp.concatenate([u.line(s, z, x0, nx) for s in range(2)], 0), self.sine)
            feed = []
            for x in range(x0, x0 + nx):
                line = self.held[(z // 4) * 3 + x // 16, 2, self.natural(z % 4), pl.ds(x % 16, 1), :]
                feed.append(jnp.broadcast_to(line, (8, WIDE)))
            feed = jnp.concatenate(feed, 0)
            p, q = real[: nx * 8], real[nx * 8 :]
            self.reals[place][0 : nx * 8, :] = (1.0 + p) * (q + p * (feed + q))

        def modes(place):
            self.modes[place][0 : nx * 8, :] = transform(self.reals[place][0 : nx * 8, :], self.sine_tenth)

        def sums(i, place):
            z = right.z0 + i
            row = [{x: u.get(s, z, x) for x in range(x0 - 1, x0 + nx + 1)} for s in range(2)]
            half = lax.div(z - 4, 8)
            line = z - 8 * half
            for x in range(x0, x0 + nx):
                laplace = []
                for s in range(2):
                    zx = (row[s][x - 1] + row[s][x + 1]) + (u.get(s, z, x, -1) + u.get(s, z, x, 1))
                    laplace.append(zx + lam6 * row[s][x])
                    if s == 0:
                        drift = zx + lam61 * row[s][x]
                n = self.modes[place][(x - x0) * 8 : (x - x0) * 8 + 8, :]
                rate.put(0, 0, x, drift + n)
                rate.put(1, 0, x, 2.0 * laplace[1] - n)
                for s in range(2):
                    integral = total([weights[s][j] * rate.row(s, 0, x, j) for j in range(M)])
                    base = inv[s] * anchor.row(0, line, x, 4 * half + s) + integral
                    right.put(s, z, x, base - a[s] * laplace[s])
                    out.put(s, z, x, base + a6[s] * row[s][x])

        nonlinear(jnp.int32(0), 0)
        nonlinear(jnp.int32(1), 1)
        modes(0)

        def body(h, _):
            for place in range(2):
                i = 2 * h + place
                nonlinear(i + 2, place)
                modes(1 - place)
                sums(i, place)
            return 0

        ready = 0
        if pause is not None:
            ready = 2
            lax.fori_loop(0, ready, body, 0)
            pause()
        lax.fori_loop(ready, lines // 2, body, 0)

    def jacobi(self, src, right, dst, sweep, lines, species):
        lam = self.co("lam")
        a = [self.co(("a", s, sweep)) for s in range(2)]

        def body(z, _):
            for x0 in range(dst.x0, dst.x0 + dst.nx, 7):
                xs = range(x0, min(x0 + 7, dst.x0 + dst.nx))
                for s in species:
                    row = {x: src.get(s, z, x) for x in range(xs[0] - 1, xs[-1] + 2)}
                    for x in xs:
                        zx = (row[x - 1] + row[x + 1]) + (src.get(s, z, x, -1) + src.get(s, z, x, 1))
                        dst.put(s, z, x, right.get(s, z, x) + a[s] * (zx + lam * row[x]))
            return 0

        lax.fori_loop(*lines, body, 0)

    def layout(self):
        powers = [Stack(self.power[0], 0, 16, 0, 48)]
        powers += [Stack(self.power[i], i, 16 - 2 * i, 4 + i, 40 - 2 * i) for i in range(1, 5)]
        return powers, Stack(self.state[0], *span(8))

    def iterate(self, out, right, sweep, depth, dst, species=(0, 1)):
        for d, place in ((depth - 2, 3), (depth - 3, 2), (depth - 4, None)):
            to = dst if place is None else Stack(self.state[place], *span(d))
            self.zero_edges(out, species)
            z0, layers, _, _ = span(d)
            self.jacobi(out, right, to, sweep, (z0, z0 + layers), species)
            out = to

    def step(self, half, share):
        powers, u = self.layout()
        for i in range(4):
            self.zero_packed(powers[i])
            self.apply_s(powers[i], powers[i + 1])
        self.combine(powers, u)
        right, out = Stack(self.state[1], *span(7)), Stack(self.state[2], *span(7))
        self.zero_edges(u)
        self.rates(u, powers[0], right, out, 2)
        u = self.second(half)
        self.iterate(out, right, 2, 8, u)
        self.zero_edges(u, lines=(Z_AT - 4, Z_AT + OWN_Z))
        pause = share(u)
        right, out = Stack(self.state[1], *span(3)), Stack(self.state[2], *span(3))
        self.rates(u, powers[0], right, out, 3, pause)
        return right, out, Stack(self.state[0], *span(0))

    def second(self, half):
        return Stack(half, Z_AT - 4, 12, X_AT - 4, OWN_X + 8)


def strip_of(node):
    y = node // 2
    return 2 * y + (node + y) % 2


class Links:
    def __init__(self):
        self.sent = []

    def send(self, when, copy):
        @pl.when(when)
        def _():
            copy.start()

        self.sent.append((when, copy))

    def finish(self):
        for when, copy in self.sent:

            @pl.when(when)
            def _():
                copy.wait_send()


def remote(src, dst, sent, got, node, g):
    return pltpu.make_async_remote_copy(
        src_ref=src, dst_ref=dst, send_sem=sent, recv_sem=got, device_id=(node, g), device_id_type=MESH
    )


def arrive(when, copy):
    @pl.when(when)
    def _():
        copy.wait_recv()


def exchange(held, sems, n, g, k, own_parts, strips_too, load):
    zs, zr, xs, xr, ss, sr = sems
    links = Links()
    tau = 2 * (g % 2) - 1
    partner = g - tau
    low, high = k > 0, k < STRIPS - 1

    def inside(i):
        return jnp.logical_and(i >= 0, i < SLABS)

    def block(slot, strip):
        return held.at[slot * 3 + strip]

    for d, away in ((1, tau), (2, -2 * tau), (3, 3 * tau)):
        for i, (src, part) in enumerate(own_parts):
            copy = remote(src, held.at[(3 - d) * 3 + 1, part], zs.at[d - 1, i], zr.at[d - 1, i], n, g + away)
            links.send(inside(g + away), copy)

    def along_x(j, there):
        for way, (ok, to, strip) in enumerate(((high, k + 1, 0), (low, k - 1, 2))):
            copy = remote(block(3 - j, 1), block(3 - j, strip), xs.at[j, way], xr.at[j, way], strip_of(to), g)
            links.send(jnp.logical_and(ok, there), copy)

    def swap(j, strip, there):
        copy = remote(block(3 - j, strip), block(4 + j, strip), ss.at[j, strip], sr.at[j, strip], n, partner)
        links.send(there, copy)

    def from_z(j):
        there = inside(g + tau * j)
        for i, (src, part) in enumerate(own_parts):
            arrive(there, remote(src, held.at[(3 - j) * 3 + 1, part], zs.at[j - 1, i], zr.at[j - 1, i], n, partner))
        along_x(j, there)
        if j < 2:
            swap(j, 1, there)

    def from_x(j):
        there = inside(g + tau * j)
        for way, (ok, strip) in enumerate(((low, 0), (high, 2))):
            when = jnp.logical_and(ok, there)
            got = block(3 - j, strip)
            arrive(when, remote(got, got, xs.at[j, way], xr.at[j, way], n, partner))
            if j < 2:
                swap(j, strip, when)

    def from_partner(j):
        there = inside(g - tau * (j + 1))
        for strip, ok in ((0, low), (1, always), (2, high)):
            got = block(4 + j, strip)
            arrive(jnp.logical_and(ok, there), remote(got, got, ss.at[j, strip], sr.at[j, strip], n, partner))

    always = g >= 0
    swap(0, 1, always)
    if strips_too:
        along_x(0, always)
        from_x(0)
        from_z(1)
        load(3)
    else:
        swap(0, 0, low)
        swap(0, 2, high)
        load(3)
        from_z(1)
    from_z(2)
    from_z(3)
    from_x(1)
    from_partner(0)
    load(2)
    load(4)
    from_x(2)
    load(1)
    from_partner(1)
    load(5)
    from_x(3)
    load(0)
    links.finish()


def refs_of(held, consts, scratch):
    sine, sine_tenth, coef = consts
    return dict(
        held=held, sine=sine, sine_tenth=sine_tenth, coef=coef,
        power=scratch[0:5], state=scratch[5:9], rate=scratch[9], reals=scratch[10:12], modes=scratch[12:14],
    )


def constants():
    return wide(SINE), wide(0.1 * SINE), COEF


def compute_scratch():
    f32 = jnp.float32
    scratch = [pltpu.VMEM((16 * 48 * 8, WIDE), f32)]
    scratch += [pltpu.VMEM(((16 - 2 * i) * (40 - 2 * i) * 8, WIDE), f32) for i in range(1, 5)]
    scratch += [pltpu.VMEM((volume(d), WIDE), f32) for d in (8, 7, 7, 6)]
    return scratch + [pltpu.VMEM((2 * 30 * 8, WIDE), f32)] + [pltpu.VMEM((30 * 8, WIDE), f32)] * 4 + [pltpu.VMEM((2 * 12 * 24 * 8, WIDE), f32)] * 2


def kernel(initial, feed, *rest):
    consts, (out, held, later, rows, sending) = rest[0:3], rest[3:8]
    scratch, sems = rest[8:-19], rest[-19:]
    sine = consts[0]
    own_sem, first_sems, second_sems, (send_sem, recv_sem), shares = sems[0], sems[1:7], sems[7:13], sems[13:15], sems[15:19]
    n, g = lax.axis_index("node"), lax.axis_index("gz")
    k = strip_of(n)
    tau = 2 * (g % 2) - 1

    barrier = pltpu.get_barrier_semaphore()
    count = M - 1
    for j in range(1, M):
        pl.semaphore_signal(barrier, inc=1, device_id=((n + j) % M, g), device_id_type=MESH)
    for away in (-2 * tau, -tau, tau, 2 * tau, 3 * tau):
        there = jnp.logical_and(g + away >= 0, g + away < SLABS)
        count = count + jnp.where(there, 1, 0)

        @pl.when(there)
        def _():
            pl.semaphore_signal(barrier, inc=1, device_id=(n, g + away), device_id_type=MESH)

    own = []
    for strip, ok in ((0, k > 0), (1, k >= 0), (2, k < STRIPS - 1)):
        rows_of = pl.ds(pl.multiple_of(OWN_X * (k + strip - 1), 16), OWN_X)
        for i, (src, part) in enumerate(((initial.at[:, :, rows_of, :], pl.ds(0, 2)), (feed.at[:, rows_of, :], 2))):
            own.append((ok, pltpu.make_async_copy(src, held.at[9 + strip, part], own_sem.at[strip, i])))
    for ok, copy in own:

        @pl.when(ok)
        def _():
            copy.start()

    pl.semaphore_wait(barrier, count)
    for ok, copy in own:

        @pl.when(ok)
        def _():
            copy.wait()

    device = Device(refs_of(held, consts, scratch), g, k)
    powers, _ = device.layout()

    def load(blocks, first):
        return lambda slot: device.load(blocks, first, powers[0], slot)

    parts = pl.ds(0, 3)
    exchange(held, first_sems, n, g, k, ((held.at[10, parts], parts),), False, load(held, True))
    halves = scratch[14:16]

    def share(i):
        def start(u):
            copies = []
            for s in range(2):
                for z in range(OWN_Z):
                    src = u.ref.at[pl.ds(u.at(s, Z_AT + z, u.x0), u.nx * 8), :]
                    dst = u.ref.at[pl.ds(u.at(s, Z_AT + 7 - z, u.x0), u.nx * 8), :]
                    place = s * OWN_Z + z
                    copies.append(remote(src, dst, shares[2 * i].at[place], shares[2 * i + 1].at[place], n, g - tau))
            for copy in copies:
                copy.start()

            def wait():
                for copy in copies:
                    copy.wait()

            return wait

        return start

    right, iterate, u = device.step(halves[0], share(0))
    device.iterate(iterate, right, 3, 4, u)
    for s in range(2):
        for z in range(OWN_Z):
            for t in range(2):
                at = u.at(s, Z_AT + device.natural(z), X_AT + 8 * t)
                later[10, s, z, 8 * t : 8 * t + 8, :] = u.ref[pl.ds(at + M - 1, 8, stride=8), :]
    parts = pl.ds(0, 2)
    exchange(later, second_sems, n, g, k, ((later.at[10, parts], parts),), True, load(later, False))

    right, iterate, u = device.step(halves[1], share(1))
    copies = []
    for s in range(2):
        device.iterate(iterate, right, 3, 4, u, (s,))
        rows[...] = transform(u.ref[s * volume(0) // 2 : (s + 1) * volume(0) // 2, :], sine)

        def spread(m, _):
            for z in range(OWN_Z):
                for t in range(2):
                    at = pl.multiple_of((device.natural(z) * OWN_X + 8 * t) * 8, 8)
                    sending[m, s, z, 8 * t : 8 * t + 8, :] = rows[pl.ds(at + m, 8, stride=8), :]
            return 0

        lax.fori_loop(0, M, spread, 0)
        here = out.at[0, s, :, pl.ds(pl.multiple_of(OWN_X * k, 16), OWN_X), :]
        for j in (4, 3, 5, 2, 6, 1, 7):
            to = (n + j) % M
            copies.append(remote(sending.at[to, s], here, send_sem.at[s, j], recv_sem.at[s, j], to, g))
            copies[-1].start()
        copies.append(pltpu.make_async_copy(sending.at[n, s], here, send_sem.at[s, 0]))
        copies[-1].start()
    for copy in copies:
        copy.wait()


def on_device(initial, feed):
    sem = pltpu.SemaphoreType.DMA
    f32 = jnp.float32
    exchanges = [sem((3, 1)), sem((3, 1)), sem((4, 2)), sem((4, 2)), sem((2, 3)), sem((2, 3))]
    scratch = [
        pltpu.VMEM((3 * SLOTS, 3, OWN_Z, OWN_X, WIDE), f32),
        pltpu.VMEM((3 * SLOTS, 2, OWN_Z, OWN_X, WIDE), f32),
        pltpu.VMEM((volume(0) // 2, WIDE), f32),
        pltpu.VMEM((M, 2, OWN_Z, OWN_X, WIDE), f32),
    ]
    scratch += compute_scratch()
    scratch += [sem((3, 2))] + exchanges + exchanges + [sem((2, M)), sem((2, M))] + [sem((2 * OWN_Z,))] * 4
    vmem, anywhere = pl.BlockSpec(memory_space=pltpu.VMEM), pl.BlockSpec(memory_space=pl.ANY)
    return pl.pallas_call(
        kernel,
        out_shape=jax.ShapeDtypeStruct((1, 2, OWN_Z, WIDE, WIDE), f32),
        in_specs=[anywhere, anywhere] + [vmem] * 3,
        out_specs=anywhere,
        scratch_shapes=scratch,
        compiler_params=pltpu.CompilerParams(
            collective_id=0, has_side_effects=True, vmem_limit_bytes=60 * 1024 * 1024
        ),
    )(initial, feed, *[jnp.asarray(c) for c in constants()])


def solution(mesh):
    in_specs = (P(None, "gz", None, None), P("gz", None, None))
    out_specs = P("node", None, "gz", None, None)
    return jax.shard_map(on_device, mesh=mesh, in_specs=in_specs, out_specs=out_specs, check_vma=False)
```

```python
import math

import jax
import jax.numpy as jnp
import ml_dtypes
import numpy as np
from jax import lax
from jax.experimental import pallas as pl
from jax.experimental.pallas import tpu as pltpu
from jax.sharding import PartitionSpec as P

MESH = pl.DeviceIdType.MESH
M = 8
SLABS, STRIPS = 32, 8
OWN_Z, OWN_X = 4, 16
Z_AT, X_AT = 12, 16
SLOTS = 6
WIDE = 128


def legendre_pair(count, point):
    before = 1.0
    current = point
    for order in range(2, count + 1):
        after = ((2.0 * order - 1.0) * point * current - (order - 1.0) * before) / order
        before = current
        current = after
    return (current, before)


def radau_value(count, point):
    high, low = legendre_pair(count, point)
    return high - low


def radau_slope(count, point):
    high, low = legendre_pair(count, point)
    lower_high, lower_low = legendre_pair(count - 1, point)
    denom = point * point - 1.0
    slope_high = count * (point * high - low) / denom
    slope_low = (count - 1.0) * (point * lower_high - lower_low) / denom
    return slope_high - slope_low


def radau_tables(node_count):
    points = [1.0]
    for index in range(1, node_count):
        guess = math.cos(2.0 * math.pi * index / (2.0 * node_count - 1.0))
        for newton_index in range(100):
            guess = guess - radau_value(node_count, guess) / radau_slope(node_count, guess)
        points.append(guess)
    points = sorted(points)
    nodes = [(value + 1.0) / 2.0 for value in points]
    table = []
    for row in range(node_count):
        table.append([0.0] * node_count)
    for column in range(node_count):
        coeffs = [1.0]
        for other in range(node_count):
            if other != column:
                factor = 1.0 / (nodes[column] - nodes[other])
                shifted = [0.0] + coeffs
                scaled = [-nodes[other] * value for value in coeffs] + [0.0]
                coeffs = [(shifted[k] + scaled[k]) * factor for k in range(len(shifted))]
        for row in range(node_count):
            total = 0.0
            for power in range(len(coeffs)):
                total = total + coeffs[power] * nodes[row] ** (power + 1) / (power + 1.0)
            table[row][column] = total
    return (nodes, table)


def tables():
    nodes, weights = radau_tables(M)
    t, q = np.asarray(nodes), np.asarray(weights)
    k = np.arange(1, WIDE + 1)
    sine = np.sqrt(2.0 / (WIDE + 1)) * np.sin(np.pi * np.outer(k, k) / (WIDE + 1))
    index, rows = {}, []

    def add(name, column):
        index[name] = len(rows)
        rows.append(np.broadcast_to(column[:, None], (8, WIDE)))

    index["lam"] = 0
    rows.append(np.broadcast_to(2.0 * np.cos(np.pi * k / (WIDE + 1))[None, :], (8, WIDE)))
    for s, nu in ((0, 1.0), (1, 2.0)):
        c = t * nu
        i = 1.0 / (1.0 + 6.0 * c)
        a = c * i
        for p in range(4):
            add(("A", s, p), a**p * i * ((1.0 - 0.1 * t) if s == 0 else 1.0))
            add(("N", s, p), a**p * i * t * (1.0 if s == 0 else -1.0))
        add(("A", s, 4), a**4)
        for sweep in (2, 3):
            c = t * nu / sweep
            i = 1.0 / (1.0 + 6.0 * c)
            add(("i", s, sweep), i)
            add(("a", s, sweep), c * i)
            for j in range(M):
                add(("q", s, sweep, j), i * q[:, j])
    return np.concatenate(rows, 0).astype(np.float32), index, sine


COEF, INDEX, SINE = tables()


def wide(matrix):
    high = matrix.astype(ml_dtypes.bfloat16)
    low = (matrix - high.astype(np.float64)).astype(ml_dtypes.bfloat16)
    return np.block([[high, low], [high, np.zeros_like(low)]]).astype(ml_dtypes.bfloat16)


def transform(v, matrix):
    high = v.astype(jnp.bfloat16)
    low = (v - high.astype(jnp.float32)).astype(jnp.bfloat16)
    both = jnp.dot(jnp.concatenate([high, low], 1), matrix[...], preferred_element_type=jnp.float32)
    return both[:, :WIDE] + both[:, WIDE:]


def total(terms):
    while len(terms) > 1:
        odd = [terms[-1]] if len(terms) % 2 else []
        terms = [terms[i] + terms[i + 1] for i in range(0, len(terms) - 1, 2)] + odd
    return terms[0]


class Stack:
    def __init__(self, ref, z0, nz, x0, nx):
        self.ref, self.z0, self.nz, self.x0, self.nx = ref, z0, nz, x0, nx
        self.lines = {}

    def start(self, s, z):
        if isinstance(z, int):
            return (s * self.nz + z - self.z0) * self.nx * 8
        if (s, id(z)) not in self.lines:
            self.lines[s, id(z)] = z, (z + (s * self.nz - self.z0)) * (self.nx * 8)
        return self.lines[s, id(z)][1]

    def at(self, s, z, x, dz=0):
        return pl.multiple_of(self.start(s, z) + (dz * self.nx + x - self.x0) * 8, 8)

    def get(self, s, z, x, dz=0):
        return self.ref[pl.ds(self.at(s, z, x, dz), 8), :]

    def put(self, s, z, x, v):
        self.ref[pl.ds(self.at(s, z, x), 8), :] = v

    def row(self, s, z, x, f):
        return jnp.broadcast_to(self.ref[pl.ds(self.at(s, z, x) + f, 1), :], (8, WIDE))

    def line(self, s, z, x, n):
        return self.ref[pl.ds(self.at(s, z, x), n * 8), :]


def span(depth):
    layers = OWN_Z + (2 * depth if depth < 4 else depth + (depth - 4))
    return (Z_AT - depth, layers, X_AT - depth, OWN_X + 2 * depth)


def volume(depth):
    _, layers, _, columns = span(depth)
    return 2 * layers * columns * 8


class Device:
    def __init__(self, refs, g, k):
        self.__dict__.update(refs)
        self.k, self.core = k, g % 2
        self.far = g // 2 + self.core * (SLABS // 2 - 1 - 2 * (g // 2))

    def zero_packed(self, stack):
        for edge, x in ((0, X_AT - 1), (STRIPS - 1, X_AT + OWN_X)):

            @pl.when(self.k == edge)
            def _():
                def body(z, _):
                    stack.put(0, z, x, jnp.zeros((8, WIDE), jnp.float32))
                    return 0

                lax.fori_loop(stack.z0, stack.z0 + stack.nz, body, 0)

        for edge, z in ((0, Z_AT - 1), (1, Z_AT - 9), (SLABS // 2 - 1, Z_AT + 8)):

            @pl.when(self.far == edge)
            def _():
                for half in range(2):
                    line = z - 8 * half
                    if stack.z0 <= line < stack.z0 + stack.nz:

                        def body(x, _):
                            stack.ref[pl.ds(stack.at(0, line, x) + 4 * half, 4), :] = jnp.zeros((4, WIDE), jnp.float32)
                            return 0

                        lax.fori_loop(stack.x0, stack.x0 + stack.nx, body, 0)

    def natural(self, layer):
        return layer + self.core * (OWN_Z - 1 - 2 * layer)

    def co(self, name):
        i = INDEX[name]
        return self.coef[i * 8 : (i + 1) * 8, :]

    def zero_edges(self, stack, species=(0, 1), lines=None):
        first, last = lines or (stack.z0, stack.z0 + stack.nz)
        for edge, x in ((0, X_AT - 1), (STRIPS - 1, X_AT + OWN_X)):

            @pl.when(self.k == edge)
            def _():
                def body(z, _):
                    for s in species:
                        stack.put(s, z, x, jnp.zeros((8, WIDE), jnp.float32))
                    return 0

                lax.fori_loop(first, last, body, 0)

        for edge, z in ((0, Z_AT - 1), (1, Z_AT - 9), (SLABS // 2 - 1, Z_AT + 8)):
            if first <= z < last:

                @pl.when(self.far == edge)
                def _():
                    for s in species:
                        stack.ref[pl.ds(stack.at(s, z, stack.x0), stack.nx * 8), :] = jnp.zeros(
                            (stack.nx * 8, WIDE), jnp.float32
                        )

    def load(self, blocks, first, stack, slot):
        b = slot * 3
        x = jnp.concatenate([blocks[b + i, 0:2].reshape(128, WIDE) for i in range(3)], 0)
        y = transform(x, self.sine)
        real, spec = (x, y) if first else (y, x)
        n = []
        for i in range(3):
            p, q = real[i * 128 : i * 128 + 64], real[i * 128 + 64 : i * 128 + 128]
            feed = self.held[b + i, 2].reshape(64, WIDE)
            n.append((1.0 + p) * (q + p * (feed + q)))
        n = transform(jnp.concatenate(n, 0), self.sine_tenth)
        for half in range(2):
            if not 0 <= slot - 2 * half < 4:
                continue
            for i in range(3):
                for layer in range(4):
                    for t in range(2):
                        z = (slot - 2 * half) * 4 + self.natural(layer)
                        at = stack.at(0, z, i * 16 + t * 8) + 4 * half
                        r = layer * 16 + t * 8
                        for f, v in (
                            (0, spec[i * 128 + r : i * 128 + r + 8]),
                            (1, spec[i * 128 + 64 + r : i * 128 + 64 + r + 8]),
                            (2, n[i * 64 + r : i * 64 + r + 8]),
                        ):
                            stack.ref[pl.ds(at + f, 8, stride=8), :] = v

    def apply_s(self, src, dst):
        lam = self.co("lam")

        def body(z, _):
            for x0 in range(dst.x0, dst.x0 + dst.nx, 8):
                xs = range(x0, min(x0 + 8, dst.x0 + dst.nx))
                row = {x: src.get(0, z, x) for x in range(xs[0] - 1, xs[-1] + 2)}
                for x in xs:
                    zx = (row[x - 1] + row[x + 1]) + (src.get(0, z, x, -1) + src.get(0, z, x, 1))
                    dst.put(0, z, x, zx + lam * row[x])
            return 0

        lax.fori_loop(dst.z0, dst.z0 + dst.nz, body, 0)

    def combine(self, powers, out):
        ca = [[self.co(("A", s, p)) for p in range(5)] for s in range(2)]
        cn = [[self.co(("N", s, p)) for p in range(4)] for s in range(2)]
        def body(z, _):
            half = lax.div(z - 4, 8)
            line, row = z - 8 * half, 4 * half
            for x in range(out.x0, out.x0 + out.nx):
                n = [powers[p].row(0, line, x, row + 2) for p in range(4)]
                for s in range(2):
                    terms = [ca[s][p] * powers[p].row(0, line, x, row + s) for p in range(5)]
                    out.put(s, z, x, total(terms + [cn[s][p] * n[p] for p in range(4)]))
            return 0

        lax.fori_loop(out.z0, out.z0 + out.nz, body, 0)

    def rates(self, u, anchor, right, out, sweep, pause=None):
        lam = self.co("lam")
        a, inv = [[self.co((name, s, sweep)) for s in range(2)] for name in "ai"]
        a6 = [6.0 * a[s] for s in range(2)]
        weights = [[self.co(("q", s, sweep, j)) for j in range(M)] for s in range(2)]
        nx, x0, lines = right.nx, right.x0, right.nz
        lam6, lam61 = lam - 6.0, lam - 6.1
        rate = Stack(self.rate, 0, 1, x0, nx)

        def nonlinear(i, place):
            z = right.z0 + lax.rem(i, lines)
            real = transform(jnp.concatenate([u.line(s, z, x0, nx) for s in range(2)], 0), self.sine)
            feed = []
            for x in range(x0, x0 + nx):
                line = self.held[(z // 4) * 3 + x // 16, 2, self.natural(z % 4), pl.ds(x % 16, 1), :]
                feed.append(jnp.broadcast_to(line, (8, WIDE)))
            feed = jnp.concatenate(feed, 0)
            p, q = real[: nx * 8], real[nx * 8 :]
            self.reals[place][0 : nx * 8, :] = (1.0 + p) * (q + p * (feed + q))

        def modes(place):
            self.modes[place][0 : nx * 8, :] = transform(self.reals[place][0 : nx * 8, :], self.sine_tenth)

        def sums(i, place):
            z = right.z0 + i
            row = [{x: u.get(s, z, x) for x in range(x0 - 1, x0 + nx + 1)} for s in range(2)]
            half = lax.div(z - 4, 8)
            line = z - 8 * half
            for x in range(x0, x0 + nx):
                laplace = []
                for s in range(2):
                    zx = (row[s][x - 1] + row[s][x + 1]) + (u.get(s, z, x, -1) + u.get(s, z, x, 1))
                    laplace.append(zx + lam6 * row[s][x])
                    if s == 0:
                        drift = zx + lam61 * row[s][x]
                n = self.modes[place][(x - x0) * 8 : (x - x0) * 8 + 8, :]
                rate.put(0, 0, x, drift + n)
                rate.put(1, 0, x, 2.0 * laplace[1] - n)
                for s in range(2):
                    integral = total([weights[s][j] * rate.row(s, 0, x, j) for j in range(M)])
                    base = inv[s] * anchor.row(0, line, x, 4 * half + s) + integral
                    right.put(s, z, x, base - a[s] * laplace[s])
                    out.put(s, z, x, base + a6[s] * row[s][x])

        nonlinear(jnp.int32(0), 0)
        nonlinear(jnp.int32(1), 1)
        modes(0)

        def body(h, _):
            for place in range(2):
                i = 2 * h + place
                nonlinear(i + 2, place)
                modes(1 - place)
                sums(i, place)
            return 0

        ready = 0
        if pause is not None:
            ready = 2
            lax.fori_loop(0, ready, body, 0)
            pause()
        lax.fori_loop(ready, lines // 2, body, 0)

    def jacobi(self, src, right, dst, sweep, lines, species):
        lam = self.co("lam")
        a = [self.co(("a", s, sweep)) for s in range(2)]

        def body(z, _):
            for x0 in range(dst.x0, dst.x0 + dst.nx, 7):
                xs = range(x0, min(x0 + 7, dst.x0 + dst.nx))
                for s in species:
                    row = {x: src.get(s, z, x) for x in range(xs[0] - 1, xs[-1] + 2)}
                    for x in xs:
                        zx = (row[x - 1] + row[x + 1]) + (src.get(s, z, x, -1) + src.get(s, z, x, 1))
                        dst.put(s, z, x, right.get(s, z, x) + a[s] * (zx + lam * row[x]))
            return 0

        lax.fori_loop(*lines, body, 0)

    def layout(self):
        powers = [Stack(self.power[0], 0, 16, 0, 48)]
        powers += [Stack(self.power[i], i, 16 - 2 * i, 4 + i, 40 - 2 * i) for i in range(1, 5)]
        return powers, Stack(self.state[0], *span(8))

    def iterate(self, out, right, sweep, depth, dst, species=(0, 1)):
        for d, place in ((depth - 2, 3), (depth - 3, 2), (depth - 4, None)):
            to = dst if place is None else Stack(self.state[place], *span(d))
            self.zero_edges(out, species)
            z0, layers, _, _ = span(d)
            self.jacobi(out, right, to, sweep, (z0, z0 + layers), species)
            out = to

    def step(self, half, share):
        powers, u = self.layout()
        for i in range(4):
            self.zero_packed(powers[i])
            self.apply_s(powers[i], powers[i + 1])
        self.combine(powers, u)
        right, out = Stack(self.state[1], *span(7)), Stack(self.state[2], *span(7))
        self.zero_edges(u)
        self.rates(u, powers[0], right, out, 2)
        u = self.second(half)
        self.iterate(out, right, 2, 8, u)
        self.zero_edges(u, lines=(Z_AT - 4, Z_AT + OWN_Z))
        pause = share(u)
        right, out = Stack(self.state[1], *span(3)), Stack(self.state[2], *span(3))
        self.rates(u, powers[0], right, out, 3, pause)
        return right, out, Stack(self.state[0], *span(0))

    def second(self, half):
        return Stack(half, Z_AT - 4, 12, X_AT - 4, OWN_X + 8)


def strip_of(node):
    y = node // 2
    return 2 * y + (node + y) % 2


class Links:
    def __init__(self):
        self.sent = []

    def send(self, when, copy):
        @pl.when(when)
        def _():
            copy.start()

        self.sent.append((when, copy))

    def finish(self):
        for when, copy in self.sent:

            @pl.when(when)
            def _():
                copy.wait_send()


def remote(src, dst, sent, got, node, g):
    return pltpu.make_async_remote_copy(
        src_ref=src, dst_ref=dst, send_sem=sent, recv_sem=got, device_id=(node, g), device_id_type=MESH
    )


def arrive(when, copy):
    @pl.when(when)
    def _():
        copy.wait_recv()


def exchange(held, sems, n, g, k, own_parts, strips_too, load):
    zs, zr, xs, xr, ss, sr = sems
    links = Links()
    tau = 2 * (g % 2) - 1
    partner = g - tau
    low, high = k > 0, k < STRIPS - 1

    def inside(i):
        return jnp.logical_and(i >= 0, i < SLABS)

    def block(slot, strip):
        return held.at[slot * 3 + strip]

    for d, away in ((1, tau), (2, -2 * tau), (3, 3 * tau)):
        for i, (src, part) in enumerate(own_parts):
            copy = remote(src, held.at[(3 - d) * 3 + 1, part], zs.at[d - 1, i], zr.at[d - 1, i], n, g + away)
            links.send(inside(g + away), copy)

    def along_x(j, there):
        for way, (ok, to, strip) in enumerate(((high, k + 1, 0), (low, k - 1, 2))):
            copy = remote(block(3 - j, 1), block(3 - j, strip), xs.at[j, way], xr.at[j, way], strip_of(to), g)
            links.send(jnp.logical_and(ok, there), copy)

    def swap(j, strip, there):
        copy = remote(block(3 - j, strip), block(4 + j, strip), ss.at[j, strip], sr.at[j, strip], n, partner)
        links.send(there, copy)

    def from_z(j):
        there = inside(g + tau * j)
        for i, (src, part) in enumerate(own_parts):
            arrive(there, remote(src, held.at[(3 - j) * 3 + 1, part], zs.at[j - 1, i], zr.at[j - 1, i], n, partner))
        along_x(j, there)
        if j < 2:
            swap(j, 1, there)

    def from_x(j):
        there = inside(g + tau * j)
        for way, (ok, strip) in enumerate(((low, 0), (high, 2))):
            when = jnp.logical_and(ok, there)
            got = block(3 - j, strip)
            arrive(when, remote(got, got, xs.at[j, way], xr.at[j, way], n, partner))
            if j < 2:
                swap(j, strip, when)

    def from_partner(j):
        there = inside(g - tau * (j + 1))
        for strip, ok in ((0, low), (1, always), (2, high)):
            got = block(4 + j, strip)
            arrive(jnp.logical_and(ok, there), remote(got, got, ss.at[j, strip], sr.at[j, strip], n, partner))

    always = g >= 0
    swap(0, 1, always)
    if strips_too:
        along_x(0, always)
        from_x(0)
        from_z(1)
        load(3)
    else:
        swap(0, 0, low)
        swap(0, 2, high)
        load(3)
        from_z(1)
    from_z(2)
    from_z(3)
    from_x(1)
    from_partner(0)
    load(2)
    load(4)
    from_x(2)
    load(1)
    from_partner(1)
    load(5)
    from_x(3)
    load(0)
    links.finish()


def refs_of(held, consts, scratch):
    sine, sine_tenth, coef = consts
    return dict(
        held=held, sine=sine, sine_tenth=sine_tenth, coef=coef,
        power=scratch[0:5], state=scratch[5:9], rate=scratch[9], reals=scratch[10:12], modes=scratch[12:14],
    )


def constants():
    return wide(SINE), wide(0.1 * SINE), COEF


def compute_scratch():
    f32 = jnp.float32
    scratch = [pltpu.VMEM((16 * 48 * 8 + 8, WIDE), f32)]
    scratch += [pltpu.VMEM(((16 - 2 * i) * (40 - 2 * i) * 8, WIDE), f32) for i in range(1, 5)]
    scratch += [pltpu.VMEM((volume(d), WIDE), f32) for d in (8, 7, 7, 6)]
    return scratch + [pltpu.VMEM((2 * 30 * 8, WIDE), f32)] + [pltpu.VMEM((30 * 8, WIDE), f32)] * 4 + [pltpu.VMEM((2 * 12 * 24 * 8, WIDE), f32)] * 2


def kernel(initial, feed, *rest):
    consts, (out, held, later, rows, sending) = rest[0:3], rest[3:8]
    scratch, sems = rest[8:-19], rest[-19:]
    sine = consts[0]
    own_sem, first_sems, second_sems, (send_sem, recv_sem), shares = sems[0], sems[1:7], sems[7:13], sems[13:15], sems[15:19]
    n, g = lax.axis_index("node"), lax.axis_index("gz")
    k = strip_of(n)
    tau = 2 * (g % 2) - 1

    barrier = pltpu.get_barrier_semaphore()
    count = M - 1
    for j in range(1, M):
        pl.semaphore_signal(barrier, inc=1, device_id=((n + j) % M, g), device_id_type=MESH)
    for away in (-2 * tau, -tau, tau, 2 * tau, 3 * tau):
        there = jnp.logical_and(g + away >= 0, g + away < SLABS)
        count = count + jnp.where(there, 1, 0)

        @pl.when(there)
        def _():
            pl.semaphore_signal(barrier, inc=1, device_id=(n, g + away), device_id_type=MESH)

    own = []
    for strip, ok in ((0, k > 0), (1, k >= 0), (2, k < STRIPS - 1)):
        rows_of = pl.ds(pl.multiple_of(OWN_X * (k + strip - 1), 16), OWN_X)
        for i, (src, part) in enumerate(((initial.at[:, :, rows_of, :], pl.ds(0, 2)), (feed.at[:, rows_of, :], 2))):
            own.append((ok, pltpu.make_async_copy(src, held.at[9 + strip, part], own_sem.at[strip, i])))
    for ok, copy in own:

        @pl.when(ok)
        def _():
            copy.start()

    pl.semaphore_wait(barrier, count)
    for ok, copy in own:

        @pl.when(ok)
        def _():
            copy.wait()

    device = Device(refs_of(held, consts, scratch), g, k)
    powers, _ = device.layout()

    def load(blocks, first):
        return lambda slot: device.load(blocks, first, powers[0], slot)

    parts = pl.ds(0, 3)
    exchange(held, first_sems, n, g, k, ((held.at[10, parts], parts),), False, load(held, True))
    halves = scratch[14:16]

    def share(i):
        def start(u):
            copies = []
            for s in range(2):
                for z in range(OWN_Z):
                    src = u.ref.at[pl.ds(u.at(s, Z_AT + z, u.x0), u.nx * 8), :]
                    dst = u.ref.at[pl.ds(u.at(s, Z_AT + 7 - z, u.x0), u.nx * 8), :]
                    place = s * OWN_Z + z
                    copies.append(remote(src, dst, shares[2 * i].at[place], shares[2 * i + 1].at[place], n, g - tau))
            for copy in copies:
                copy.start()

            def wait():
                for copy in copies:
                    copy.wait()

            return wait

        return start

    right, iterate, u = device.step(halves[0], share(0))
    device.iterate(iterate, right, 3, 4, u)
    for s in range(2):
        for z in range(OWN_Z):
            for t in range(2):
                at = u.at(s, Z_AT + device.natural(z), X_AT + 8 * t)
                later[10, s, z, 8 * t : 8 * t + 8, :] = u.ref[pl.ds(at + M - 1, 8, stride=8), :]
    parts = pl.ds(0, 2)
    exchange(later, second_sems, n, g, k, ((later.at[10, parts], parts),), True, load(later, False))

    right, iterate, u = device.step(halves[1], share(1))
    copies = []
    for s in range(2):
        device.iterate(iterate, right, 3, 4, u, (s,))
        rows[0 : volume(0) // 2, :] = transform(u.ref[s * volume(0) // 2 : (s + 1) * volume(0) // 2, :], sine)

        def spread(m, _):
            for z in range(OWN_Z):
                for t in range(2):
                    at = pl.multiple_of((device.natural(z) * OWN_X + 8 * t) * 8, 8)
                    sending[m, s, z, 8 * t : 8 * t + 8, :] = rows[pl.ds(at + m, 8, stride=8), :]
            return 0

        lax.fori_loop(0, M, spread, 0)
        here = out.at[0, s, :, pl.ds(pl.multiple_of(OWN_X * k, 16), OWN_X), :]
        for j in (4, 3, 5, 2, 6, 1, 7):
            to = (n + j) % M
            copies.append(remote(sending.at[to, s], here, send_sem.at[s, j], recv_sem.at[s, j], to, g))
            copies[-1].start()
        copies.append(pltpu.make_async_copy(sending.at[n, s], here, send_sem.at[s, 0]))
        copies[-1].start()
    for copy in copies:
        copy.wait()


def on_device(initial, feed):
    sem = pltpu.SemaphoreType.DMA
    f32 = jnp.float32
    exchanges = [sem((3, 1)), sem((3, 1)), sem((4, 2)), sem((4, 2)), sem((2, 3)), sem((2, 3))]
    scratch = [
        pltpu.VMEM((3 * SLOTS, 3, OWN_Z, OWN_X, WIDE), f32),
        pltpu.VMEM((3 * SLOTS, 2, OWN_Z, OWN_X, WIDE), f32),
        pltpu.VMEM((volume(0) // 2 + 8, WIDE), f32),
        pltpu.VMEM((M, 2, OWN_Z, OWN_X, WIDE), f32),
    ]
    scratch += compute_scratch()
    scratch += [sem((3, 2))] + exchanges + exchanges + [sem((2, M)), sem((2, M))] + [sem((2 * OWN_Z,))] * 4
    vmem, anywhere = pl.BlockSpec(memory_space=pltpu.VMEM), pl.BlockSpec(memory_space=pl.ANY)
    return pl.pallas_call(
        kernel,
        out_shape=jax.ShapeDtypeStruct((1, 2, OWN_Z, WIDE, WIDE), f32),
        in_specs=[anywhere, anywhere] + [vmem] * 3,
        out_specs=anywhere,
        scratch_shapes=scratch,
        compiler_params=pltpu.CompilerParams(
            collective_id=0, has_side_effects=True, vmem_limit_bytes=60 * 1024 * 1024
        ),
    )(initial, feed, *[jnp.asarray(c) for c in constants()])


def solution(mesh):
    in_specs = (P(None, "gz", None, None), P("gz", None, None))
    out_specs = P("node", None, "gz", None, None)
    return jax.shard_map(on_device, mesh=mesh, in_specs=in_specs, out_specs=out_specs, check_vma=False)
```
